512 devices in a mesh: seq: 64 (over z, y), segment: 8 (over x, core).
Axes of the slice: x: 4, y: 4, z: 16, core: 2. Of those that a mesh axis runs over, the one named last changes fastest.
Arguments:
- queries: bfloat16 [8, 23552, 1024], P('segment', 'seq'), may hold values from -6 to 6
- key_rows: bfloat16 [8, 23552, 1024], P('segment', 'seq'), may hold values from -6 to 6
- value_rows: bfloat16 [8, 23552, 1024], P('segment', 'seq'), may hold values from -6 to 6
- out_weight: bfloat16 [8, 1024, 1024], P('segment'), may hold values from -0.1875 to 0.1875
Outputs:
- handed: bfloat16 [8, 23552, 1024], P('segment', 'seq')
The draws below stay inside these ranges and needn't reach their ends.
All inputs are finite; a program needn't handle non-finite values.
Results may differ from the reference program's by a relative error of at most 0.0058.
Values may be sent and summed in bfloat16 or wider, within the bound.
No kernel may reach another device: no remote copies, remote signals or barrier semaphores. Data moves between devices by JAX's collectives and lax.ppermute only.
A program may use at most 128 MiB of HBM per device.

```python
import jax
import jax.numpy as jnp
from jax import lax

D = 1024
HEADS = 8
HEAD_DIM = 128
TOK_DEV = 368
TOKENS = 23552
SEGMENTS = 8


def level_of(rng, shape, cuts, smallest, largest):
    factor_of, own = 1.0, jax.random.fold_in(rng, 6)
    for axis_at, parts in cuts:
        heights = jnp.exp(jax.random.uniform(jax.random.fold_in(own, axis_at), (parts,), jnp.float32, smallest / len(cuts), largest / len(cuts)))
        factor_of = factor_of * jnp.repeat(heights, shape[axis_at] // parts).reshape([-1 if axis == axis_at else 1 for axis in range(len(shape))])
    return factor_of


def noise(stream_key, extent, width, reach, pieces=(), held_as=jnp.bfloat16):
    factor_of = level_of(stream_key, extent, pieces, -0.22, 0.18) if pieces else 1.0
    result = jax.random.normal(stream_key, extent, jnp.float32) * width * factor_of
    return jnp.minimum(jnp.maximum(result, -reach), reach).astype(held_as)


def setup_inputs(seed: int = 0) -> dict:
    key_list = jax.random.split(jax.random.key(seed), 5)
    return {
        "queries": noise(key_list[0], (SEGMENTS, TOKENS, HEADS * HEAD_DIM), 1.0, 6.0, ((0, 8), (1, 64))),
        "key_rows": noise(key_list[1], (SEGMENTS, TOKENS, HEADS * HEAD_DIM), 1.0, 6.0, ((0, 8), (1, 64))),
        "value_rows": noise(key_list[2], (SEGMENTS, TOKENS, HEADS * HEAD_DIM), 1.0, 6.0, ((0, 8), (1, 64))),
        "out_weight": noise(key_list[3], (SEGMENTS, HEADS * HEAD_DIM, D), (HEADS * HEAD_DIM) ** -0.5, 0.1875, ((0, 8),)),
    }


epsilon = 1e-06

def one_section(operands):
    queries, key_rows, value_rows, out_weight = operands
    block_count = TOKENS // TOK_DEV

    def blocks_of(array):
        return array.astype(jnp.float32).reshape(block_count, TOK_DEV, HEADS, HEAD_DIM)
    q_blocks = blocks_of(queries)
    k_blocks = blocks_of(key_rows)
    v_blocks = blocks_of(value_rows)
    states = jnp.einsum('bthd,bthe->bhde', k_blocks, v_blocks)
    running = jnp.cumsum(states, axis=0)
    prior = jnp.concatenate([jnp.zeros_like(states[:1]), running[:-1]], axis=0)
    carried = lax.optimization_barrier(prior.astype(jnp.bfloat16)).astype(jnp.float32)
    scores = jnp.einsum('bihd,bjhd->bhij', q_blocks, k_blocks)
    row_ids = lax.broadcasted_iota(jnp.int32, (TOK_DEV, TOK_DEV), 0)
    col_ids = lax.broadcasted_iota(jnp.int32, (TOK_DEV, TOK_DEV), 1)
    causal = col_ids <= row_ids
    local_part = jnp.where(causal[None, None], scores, jnp.zeros_like(scores))
    local_part = lax.optimization_barrier(local_part.astype(jnp.bfloat16)).astype(jnp.float32)
    mixed_heads = jnp.einsum('bhij,bjhe->bihe', local_part, v_blocks) + jnp.einsum('bihd,bhde->bihe', q_blocks, carried)
    normed = mixed_heads * lax.rsqrt(lax.optimization_barrier(jnp.mean(mixed_heads * mixed_heads, axis=3, keepdims=True)) + epsilon)
    normed = normed.reshape(TOKENS, HEADS * HEAD_DIM).astype(jnp.bfloat16)
    return jnp.dot(normed, out_weight, preferred_element_type=jnp.float32).astype(jnp.bfloat16)

def reference(queries, key_rows, value_rows, out_weight):
    branch = lax.map(one_section, (queries, key_rows, value_rows, out_weight))
    return jnp.roll(branch, 1, axis=0)
```

```python
import jax
import jax.numpy as jnp
from jax import lax
from jax.experimental import pallas as pl
from jax.experimental.pallas import tpu as pltpu
from jax.sharding import PartitionSpec as P

HEADS = 8
HEAD_DIM = 128
GROUP = 16
EPSILON = 1e-06

F32 = jnp.float32
BF16 = jnp.bfloat16
VMEM = pl.BlockSpec(memory_space=pltpu.VMEM)
SMEM = pl.BlockSpec(memory_space=pltpu.SMEM)


def call(body, out_shape, args, specs, flops, nbytes, limit=24 << 20, scratch=()):
    return pl.pallas_call(
        body,
        out_shape=out_shape,
        in_specs=specs,
        out_specs=jax.tree.map(lambda _: VMEM, out_shape),
        scratch_shapes=scratch,
        compiler_params=pltpu.CompilerParams(vmem_limit_bytes=limit),
        cost_estimate=pl.CostEstimate(flops=flops, bytes_accessed=nbytes, transcendentals=0),
    )(*args)


def head(h):
    return slice(h * HEAD_DIM, (h + 1) * HEAD_DIM)


def states_kernel(k_ref, v_ref, out_ref):
    for h in range(HEADS):
        state = lax.dot_general(
            k_ref[:, head(h)], v_ref[:, head(h)], (((0,), (0,)), ((), ())), preferred_element_type=F32
        )
        out_ref[head(h), :] = state.astype(BF16)


def local_kernel(q_ref, k_ref, v_ref, out_ref):
    rows = q_ref.shape[0]
    row_ids = lax.broadcasted_iota(jnp.int32, (rows, rows), 0)
    col_ids = lax.broadcasted_iota(jnp.int32, (rows, rows), 1)
    causal = col_ids <= row_ids
    for h in range(HEADS):
        scores = lax.dot_general(
            q_ref[:, head(h)], k_ref[:, head(h)], (((1,), (1,)), ((), ())), preferred_element_type=F32
        )
        scores = jnp.where(causal, scores, 0.0).astype(BF16)
        out_ref[:, head(h)] = jnp.dot(scores, v_ref[:, head(h)], preferred_element_type=F32)


def total_kernel(slices_ref, out_ref):
    acc = slices_ref[0].astype(F32)
    for m in range(1, slices_ref.shape[0]):
        acc = acc + slices_ref[m].astype(F32)
    out_ref[...] = acc


def prefix_kernel(group_ref, slices_ref, totals_ref, out_ref):
    group = group_ref[0]
    acc = jnp.zeros(out_ref.shape[1:], F32)
    for g in range(totals_ref.shape[0] - 1):
        acc = acc + jnp.where(g < group, totals_ref[g], 0.0)
    for m in range(slices_ref.shape[0]):
        out_ref[m] = acc.astype(BF16)
        acc = acc + slices_ref[m].astype(F32)


def branch_kernel(q_ref, local_ref, carried_ref, w_ref, out_ref, normed_ref):
    for h in range(HEADS):
        mixed = local_ref[:, head(h)] + jnp.dot(
            q_ref[:, head(h)], carried_ref[head(h), :], preferred_element_type=F32
        )
        scale = lax.rsqrt(jnp.mean(mixed * mixed, axis=1, keepdims=True) + EPSILON)
        normed_ref[:, head(h)] = (mixed * scale).astype(BF16)
    out_ref[...] = jnp.dot(normed_ref[...], w_ref[...], preferred_element_type=F32).astype(BF16)


def shards(queries, key_rows, value_rows, out_weight):
    q, k, v, w = queries[0], key_rows[0], value_rows[0], out_weight[0]
    rows, width = q.shape
    blocks = lax.axis_size("seq")
    near = [[g * GROUP + m for m in range(GROUP)] for g in range(blocks // GROUP)]
    far = [[g * GROUP + m for g in range(blocks // GROUP)] for m in range(GROUP)]
    piece = (HEADS * HEAD_DIM // GROUP, HEAD_DIM)

    states = call(
        states_kernel, jax.ShapeDtypeStruct((HEADS * HEAD_DIM, HEAD_DIM), BF16), (k, v), [VMEM] * 2,
        2 * rows * width * HEAD_DIM, 2 * rows * width * 2,
    )
    slices = lax.all_to_all(states.reshape(GROUP, *piece), "seq", 0, 0, axis_index_groups=near)
    total = call(
        total_kernel, jax.ShapeDtypeStruct(piece, F32), (slices,), [VMEM], 1 << 17, 1 << 19,
    )
    totals = lax.all_gather(total, "seq", axis_index_groups=far)
    local = call(
        local_kernel, jax.ShapeDtypeStruct((rows, width), F32), (q, k, v), [VMEM] * 3,
        4 * rows * rows * width, 5 * rows * width * 2,
    )
    group = (lax.axis_index("seq") // GROUP).astype(jnp.int32).reshape(1)
    prefixes = call(
        prefix_kernel, jax.ShapeDtypeStruct((GROUP, *piece), BF16), (group, slices, totals),
        [SMEM, VMEM, VMEM], 1 << 18, 1 << 20,
    )
    carried = lax.all_to_all(prefixes, "seq", 0, 0, axis_index_groups=near).reshape(-1, HEAD_DIM)
    branch = call(
        branch_kernel, jax.ShapeDtypeStruct((rows, width), BF16), (q, local, carried, w), [VMEM] * 4,
        2 * rows * width * (width + HEAD_DIM), 6 << 20, scratch=[pltpu.VMEM((rows, width), BF16)],
    )
    size = lax.axis_size("segment")
    handed = lax.ppermute(branch, "segment", [((i - 1) % size, i) for i in range(size)])
    return handed[None]


def solution(mesh):
    return jax.shard_map(
        shards,
        mesh=mesh,
        in_specs=(
            P("segment", "seq", None),
            P("segment", "seq", None),
            P("segment", "seq", None),
            P("segment", None, None),
        ),
        out_specs=P("segment", "seq", None),
        check_vma=False,
    )
```

```python
import jax
import jax.numpy as jnp
from jax import lax
from jax.experimental import pallas as pl
from jax.experimental.pallas import tpu as pltpu
from jax.sharding import PartitionSpec as P

HEADS = 8
HEAD_DIM = 128
GROUP = 16
SLAB = 2
EPSILON = 1e-06

F32 = jnp.float32
BF16 = jnp.bfloat16
VMEM = pl.BlockSpec(memory_space=pltpu.VMEM)
SMEM = pl.BlockSpec(memory_space=pltpu.SMEM)
ANY = pl.BlockSpec(memory_space=pl.ANY)


def call(body, out_shape, args, specs, flops, nbytes, out_specs=VMEM, limit=24 << 20, scratch=()):
    return pl.pallas_call(
        body,
        out_shape=out_shape,
        in_specs=specs,
        out_specs=out_specs,
        scratch_shapes=scratch,
        compiler_params=pltpu.CompilerParams(vmem_limit_bytes=limit),
        cost_estimate=pl.CostEstimate(flops=flops, bytes_accessed=nbytes, transcendentals=0),
    )(*args)


def head(h):
    return slice(h * HEAD_DIM, (h + 1) * HEAD_DIM)


def slab_copies(sources, targets, sem):
    width = SLAB * HEAD_DIM
    return [
        [
            pltpu.make_async_copy(
                source.at[:, pl.ds(s * width, width)],
                target.at[:, pl.ds(s * width, width)],
                sem.at[s, a],
            )
            for a, (source, target) in enumerate(zip(sources, targets))
        ]
        for s in range(HEADS // SLAB)
    ]


def states_kernel(k_hbm, v_hbm, out_ref, k_ref, v_ref, sem):
    copies = slab_copies((k_hbm, v_hbm), (k_ref, v_ref), sem)
    for slab in copies:
        for copy in slab:
            copy.start()
    for h in range(HEADS):
        if h % SLAB == 0:
            for copy in copies[h // SLAB]:
                copy.wait()
        state = lax.dot_general(
            k_ref[:, head(h)], v_ref[:, head(h)], (((0,), (0,)), ((), ())), preferred_element_type=F32
        )
        out_ref[head(h), :] = state.astype(BF16)


def local_kernel(q_hbm, k_hbm, v_hbm, after_ref, out_ref, k_ref, v_ref, sem):
    del after_ref
    rows = q_hbm.shape[0]
    q_ref, local_ref = out_ref.at[pl.ds(0, rows)], out_ref.at[pl.ds(rows, rows)]
    copies = slab_copies((q_hbm, k_hbm, v_hbm), (q_ref, k_ref, v_ref), sem)
    for slab in copies:
        for copy in slab:
            copy.start()
    row_ids = lax.broadcasted_iota(jnp.int32, (rows, rows), 0)
    col_ids = lax.broadcasted_iota(jnp.int32, (rows, rows), 1)
    causal = col_ids <= row_ids
    for h in range(HEADS):
        if h % SLAB == 0:
            for copy in copies[h // SLAB]:
                copy.wait()
        scores = lax.dot_general(
            q_ref[:, head(h)], k_ref[:, head(h)], (((1,), (1,)), ((), ())), preferred_element_type=F32
        )
        scores = jnp.where(causal, scores, 0.0).astype(BF16)
        local_ref[:, head(h)] = jnp.dot(
            scores, v_ref[:, head(h)], preferred_element_type=F32
        ).astype(BF16)


def total_kernel(slices_ref, out_ref):
    acc = slices_ref[0].astype(F32)
    for m in range(1, slices_ref.shape[0]):
        acc = acc + slices_ref[m].astype(F32)
    out_ref[...] = acc


def prefix_kernel(group_ref, slices_ref, totals_ref, out_ref):
    group = group_ref[0]
    acc = jnp.zeros(out_ref.shape[1:], F32)
    for g in range(totals_ref.shape[0] - 1):
        acc = acc + jnp.where(g < group, totals_ref[g], 0.0)
    for m in range(slices_ref.shape[0]):
        out_ref[m] = acc.astype(BF16)
        acc = acc + slices_ref[m].astype(F32)


def branch_kernel(pair_ref, carried_ref, w_ref, out_ref, normed_ref):
    rows = out_ref.shape[0]
    for h in range(HEADS):
        mixed = pair_ref[rows : 2 * rows, head(h)].astype(F32) + jnp.dot(
            pair_ref[0:rows, head(h)], carried_ref[head(h), :], preferred_element_type=F32
        )
        scale = lax.rsqrt(jnp.mean(mixed * mixed, axis=1, keepdims=True) + EPSILON)
        normed_ref[:, head(h)] = (mixed * scale).astype(BF16)
    out_ref[...] = jnp.dot(normed_ref[...], w_ref[...], preferred_element_type=F32).astype(BF16)


def handed_on(array):
    size = lax.axis_size("segment")
    return lax.ppermute(array, "segment", [((i - 1) % size, i) for i in range(size)])


def shards(queries, key_rows, value_rows, out_weight):
    q, k, v, w = queries[0], key_rows[0], value_rows[0], out_weight[0]
    rows, width = q.shape
    blocks = lax.axis_size("seq")
    near = [[g * GROUP + m for m in range(GROUP)] for g in range(blocks // GROUP)]
    far = [[g * GROUP + m for g in range(blocks // GROUP)] for m in range(GROUP)]
    piece = (HEADS * HEAD_DIM // GROUP, HEAD_DIM)
    block = pltpu.VMEM((rows, width), BF16)
    sems = lambda n: pltpu.SemaphoreType.DMA((HEADS // SLAB, n))

    states = call(
        states_kernel, jax.ShapeDtypeStruct((HEADS * HEAD_DIM, HEAD_DIM), BF16), (k, v), [ANY] * 2,
        2 * rows * width * HEAD_DIM, 2 * rows * width * 2, limit=60 << 20, scratch=[block, block, sems(2)],
    )
    states_next = handed_on(states)
    pair = call(
        local_kernel, jax.ShapeDtypeStruct((2 * rows, width), BF16), (q, k, v, states), [ANY] * 4,
        4 * rows * rows * width, 5 * rows * width * 2, limit=60 << 20, scratch=[block, block, sems(3)],
    )
    states_next, w, pair = lax.optimization_barrier((states_next, w, pair))
    w_next, pair_next = handed_on(w), handed_on(pair)
    slices = lax.all_to_all(states_next.reshape(GROUP, *piece), "seq", 0, 0, axis_index_groups=near)
    total = call(
        total_kernel, jax.ShapeDtypeStruct(piece, F32), (slices,), [VMEM], 1 << 17, 1 << 19,
    )
    totals = lax.all_gather(total, "seq", axis_index_groups=far)
    group = (lax.axis_index("seq") // GROUP).astype(jnp.int32).reshape(1)
    prefixes = call(
        prefix_kernel, jax.ShapeDtypeStruct((GROUP, *piece), BF16), (group, slices, totals),
        [SMEM, VMEM, VMEM], 1 << 18, 1 << 20,
    )
    carried = lax.all_to_all(prefixes, "seq", 0, 0, axis_index_groups=near).reshape(-1, HEAD_DIM)
    branch = call(
        branch_kernel, jax.ShapeDtypeStruct((rows, width), BF16),
        (pair_next, carried, w_next), [VMEM] * 3,
        2 * rows * width * (width + HEAD_DIM), 6 << 20, scratch=[pltpu.VMEM((rows, width), BF16)],
    )
    return branch[None]


def solution(mesh):
    return jax.shard_map(
        shards,
        mesh=mesh,
        in_specs=(
            P("segment", "seq", None),
            P("segment", "seq", None),
            P("segment", "seq", None),
            P("segment", None, None),
        ),
        out_specs=P("segment", "seq", None),
        check_vma=False,
    )
```

```python
import jax
import jax.numpy as jnp
from jax import lax
from jax.experimental import pallas as pl
from jax.experimental.pallas import tpu as pltpu
from jax.sharding import PartitionSpec as P

HEADS = 8
HEAD_DIM = 128
GROUP = 16
SLAB = 4
EPSILON = 1e-06

F32 = jnp.float32
BF16 = jnp.bfloat16
VMEM = pl.BlockSpec(memory_space=pltpu.VMEM)
SMEM = pl.BlockSpec(memory_space=pltpu.SMEM)
ANY = pl.BlockSpec(memory_space=pl.ANY)


def call(body, out_shape, args, specs, flops, nbytes, out_specs=VMEM, limit=24 << 20, scratch=()):
    return pl.pallas_call(
        body,
        out_shape=out_shape,
        in_specs=specs,
        out_specs=out_specs,
        scratch_shapes=scratch,
        compiler_params=pltpu.CompilerParams(vmem_limit_bytes=limit),
        cost_estimate=pl.CostEstimate(flops=flops, bytes_accessed=nbytes, transcendentals=0),
    )(*args)


def head(h):
    return slice(h * HEAD_DIM, (h + 1) * HEAD_DIM)


def slab_copies(sources, targets, sem):
    width = SLAB * HEAD_DIM
    return [
        [
            pltpu.make_async_copy(
                source.at[:, pl.ds(s * width, width)],
                target.at[:, pl.ds(s * width, width)],
                sem.at[s, a],
            )
            for a, (source, target) in enumerate(zip(sources, targets))
        ]
        for s in range(HEADS // SLAB)
    ]


def states_kernel(k_hbm, v_hbm, out_ref, k_ref, v_ref, sem):
    copies = slab_copies((k_hbm, v_hbm), (k_ref, v_ref), sem)
    for slab in copies:
        for copy in slab:
            copy.start()
    for h in range(HEADS):
        if h % SLAB == 0:
            for copy in copies[h // SLAB]:
                copy.wait()
        state = lax.dot_general(
            k_ref[:, head(h)], v_ref[:, head(h)], (((0,), (0,)), ((), ())), preferred_element_type=F32
        )
        out_ref[head(h), :] = state.astype(BF16)


def local_kernel(q_hbm, k_hbm, v_hbm, after_ref, out_ref, k_ref, v_ref, sem):
    del after_ref
    rows = q_hbm.shape[0]
    q_ref, local_ref = out_ref.at[pl.ds(0, rows)], out_ref.at[pl.ds(rows, rows)]
    copies = slab_copies((q_hbm, k_hbm, v_hbm), (q_ref, k_ref, v_ref), sem)
    for slab in copies:
        for copy in slab:
            copy.start()
    row_ids = lax.broadcasted_iota(jnp.int32, (rows, rows), 0)
    col_ids = lax.broadcasted_iota(jnp.int32, (rows, rows), 1)
    causal = col_ids <= row_ids
    for h in range(HEADS):
        if h % SLAB == 0:
            for copy in copies[h // SLAB]:
                copy.wait()
        scores = lax.dot_general(
            q_ref[:, head(h)], k_ref[:, head(h)], (((1,), (1,)), ((), ())), preferred_element_type=F32
        )
        scores = jnp.where(causal, scores, 0.0).astype(BF16)
        local_ref[:, head(h)] = jnp.dot(
            scores, v_ref[:, head(h)], preferred_element_type=F32
        ).astype(BF16)


def total_kernel(slices_ref, out_ref):
    acc = slices_ref[0].astype(F32)
    for m in range(1, slices_ref.shape[0]):
        acc = acc + slices_ref[m].astype(F32)
    out_ref[...] = acc


def prefix_kernel(slices_ref, *refs):
    totals, out_ref = refs[:-1], refs[-1]
    acc = totals[0][...]
    for total in totals[1:]:
        acc = acc + total[...]
    for m in range(slices_ref.shape[0]):
        out_ref[m] = acc.astype(BF16)
        acc = acc + slices_ref[m].astype(F32)


def fetch_kernel(pair_hbm, out_ref, sem):
    copy = pltpu.make_async_copy(pair_hbm, out_ref, sem.at[0])
    copy.start()
    copy.wait()


def branch_kernel(pair_ref, carried_ref, w_hbm, out_hbm, normed_ref, out_ref, w_ref, w_sem, sem):
    w_copies = [
        pltpu.make_async_copy(w_hbm.at[head(h), :], w_ref.at[head(h), :], w_sem.at[h])
        for h in range(HEADS)
    ]
    for copy in w_copies:
        copy.start()
    rows = out_ref.shape[0]
    for h in range(HEADS):
        mixed = pair_ref[rows : 2 * rows, head(h)].astype(F32) + jnp.dot(
            pair_ref[0:rows, head(h)], carried_ref[head(h), :], preferred_element_type=F32
        )
        scale = lax.rsqrt(jnp.mean(mixed * mixed, axis=1, keepdims=True) + EPSILON)
        normed_ref[:, head(h)] = (mixed * scale).astype(BF16)
    for copy in w_copies:
        copy.wait()
    middle = (rows // 2 + 15) // 16 * 16
    copies = []
    for n, (low, high) in enumerate(((0, middle), (middle, rows))):
        part = pl.ds(low, high - low)
        out_ref[part, :] = jnp.dot(
            normed_ref[part, :], w_ref[...], preferred_element_type=F32
        ).astype(BF16)
        copies.append(pltpu.make_async_copy(out_ref.at[part], out_hbm.at[part], sem.at[n]))
        copies[n].start()
    for copy in copies:
        copy.wait()


def handed_on(array):
    size = lax.axis_size("segment")
    return lax.ppermute(array, "segment", [((i - 1) % size, i) for i in range(size)])


def shards(queries, key_rows, value_rows, out_weight):
    q, k, v, w = queries[0], key_rows[0], value_rows[0], out_weight[0]
    rows, width = q.shape
    blocks = lax.axis_size("seq")
    near = [[g * GROUP + m for m in range(GROUP)] for g in range(blocks // GROUP)]
    piece = (HEADS * HEAD_DIM // GROUP, HEAD_DIM)
    block = pltpu.VMEM((rows, width), BF16)
    sems = lambda n: pltpu.SemaphoreType.DMA((HEADS // SLAB, n))

    states = call(
        states_kernel, jax.ShapeDtypeStruct((HEADS * HEAD_DIM, HEAD_DIM), BF16), (k, v), [ANY] * 2,
        2 * rows * width * HEAD_DIM, 2 * rows * width * 2, limit=60 << 20, scratch=[block, block, sems(2)],
    )
    states_next = handed_on(states)
    pair = call(
        local_kernel, jax.ShapeDtypeStruct((2 * rows, width), BF16), (q, k, v, states), [ANY] * 4,
        4 * rows * rows * width, 5 * rows * width * 2, limit=60 << 20, scratch=[block, block, sems(3)],
    )
    states_next, w, pair = lax.optimization_barrier((states_next, w, pair))
    w_next, pair_next = handed_on(w), handed_on(pair)
    slices = lax.all_to_all(states_next.reshape(GROUP, *piece), "seq", 0, 0, axis_index_groups=near)
    total = call(
        total_kernel, jax.ShapeDtypeStruct(piece, F32), (slices,), [VMEM], 1 << 17, 1 << 19, limit=4 << 20,
    )
    totals = [
        lax.ppermute(total, "seq", [(i, i + d * GROUP) for i in range(blocks - d * GROUP)])
        for d in range(1, blocks // GROUP)
    ]
    prefixes = call(
        prefix_kernel, jax.ShapeDtypeStruct((GROUP, *piece), BF16), (slices, *totals),
        [VMEM] * (1 + len(totals)), 1 << 18, 1 << 20, limit=4 << 20,
    )
    carried = lax.all_to_all(prefixes, "seq", 0, 0, axis_index_groups=near).reshape(-1, HEAD_DIM)
    pair_next = call(
        fetch_kernel, jax.ShapeDtypeStruct((2 * rows, width), BF16), (pair_next,), [ANY],
        0, 4 * rows * width, limit=8 << 20, scratch=[pltpu.SemaphoreType.DMA((1,))],
    )
    branch = call(
        branch_kernel, jax.ShapeDtypeStruct((rows, width), BF16),
        (pair_next, carried, w_next), [VMEM, VMEM, ANY],
        2 * rows * width * (width + HEAD_DIM), 6 << 20, out_specs=ANY, limit=16 << 20,
        scratch=[
            block, block, pltpu.VMEM((width, width), BF16),
            pltpu.SemaphoreType.DMA((HEADS,)), pltpu.SemaphoreType.DMA((2,)),
        ],
    )
    return branch[None]


def solution(mesh):
    return jax.shard_map(
        shards,
        mesh=mesh,
        in_specs=(
            P("segment", "seq", None),
            P("segment", "seq", None),
            P("segment", "seq", None),
            P("segment", None, None),
        ),
        out_specs=P("segment", "seq", None),
        check_vma=False,
    )
```

```python
import jax
import jax.numpy as jnp
from jax import lax
from jax.experimental import pallas as pl
from jax.experimental.pallas import tpu as pltpu
from jax.sharding import PartitionSpec as P

HEADS = 8
HEAD_DIM = 128
GROUP = 16
SLAB = 4
EPSILON = 1e-06

F32 = jnp.float32
BF16 = jnp.bfloat16
VMEM = pl.BlockSpec(memory_space=pltpu.VMEM)
SMEM = pl.BlockSpec(memory_space=pltpu.SMEM)
ANY = pl.BlockSpec(memory_space=pl.ANY)


def call(body, out_shape, args, specs, flops, nbytes, out_specs=VMEM, limit=24 << 20, scratch=()):
    return pl.pallas_call(
        body,
        out_shape=out_shape,
        in_specs=specs,
        out_specs=out_specs,
        scratch_shapes=scratch,
        compiler_params=pltpu.CompilerParams(vmem_limit_bytes=limit),
        cost_estimate=pl.CostEstimate(flops=flops, bytes_accessed=nbytes, transcendentals=0),
    )(*args)


def head(h):
    return slice(h * HEAD_DIM, (h + 1) * HEAD_DIM)


def slab_copies(sources, targets, sem):
    width = SLAB * HEAD_DIM
    return [
        [
            pltpu.make_async_copy(
                source.at[:, pl.ds(s * width, width)],
                target.at[:, pl.ds(s * width, width)],
                sem.at[s, a],
            )
            for a, (source, target) in enumerate(zip(sources, targets))
        ]
        for s in range(HEADS // SLAB)
    ]


def states_kernel(k_hbm, v_hbm, out_ref, k_ref, v_ref, sem):
    copies = slab_copies((k_hbm, v_hbm), (k_ref, v_ref), sem)
    for slab in copies:
        for copy in slab:
            copy.start()
    for h in range(HEADS):
        if h % SLAB == 0:
            for copy in copies[h // SLAB]:
                copy.wait()
        state = lax.dot_general(
            k_ref[:, head(h)], v_ref[:, head(h)], (((0,), (0,)), ((), ())), preferred_element_type=F32
        )
        out_ref[head(h), :] = state.astype(BF16)


def local_kernel(q_hbm, k_hbm, v_hbm, after_ref, out_ref, k_ref, v_ref, sem):
    del after_ref
    rows = q_hbm.shape[0]
    q_ref, local_ref = out_ref.at[pl.ds(0, rows)], out_ref.at[pl.ds(rows, rows)]
    copies = slab_copies((q_hbm, k_hbm, v_hbm), (q_ref, k_ref, v_ref), sem)
    for slab in copies:
        for copy in slab:
            copy.start()
    row_ids = lax.broadcasted_iota(jnp.int32, (rows, rows), 0)
    col_ids = lax.broadcasted_iota(jnp.int32, (rows, rows), 1)
    causal = col_ids <= row_ids
    for h in range(HEADS):
        if h % SLAB == 0:
            for copy in copies[h // SLAB]:
                copy.wait()
        scores = lax.dot_general(
            q_ref[:, head(h)], k_ref[:, head(h)], (((1,), (1,)), ((), ())), preferred_element_type=F32
        )
        scores = jnp.where(causal, scores, 0.0).astype(BF16)
        local_ref[:, head(h)] = jnp.dot(
            scores, v_ref[:, head(h)], preferred_element_type=F32
        ).astype(BF16)


def total_kernel(slices_ref, out_ref):
    acc = slices_ref[0].astype(F32)
    for m in range(1, slices_ref.shape[0]):
        acc = acc + slices_ref[m].astype(F32)
    out_ref[...] = acc


def prefix_kernel(slices_ref, *refs):
    totals, out_ref = refs[:-1], refs[-1]
    acc = totals[0][...]
    for total in totals[1:]:
        acc = acc + total[...]
    for m in range(slices_ref.shape[0]):
        out_ref[m] = acc.astype(BF16)
        acc = acc + slices_ref[m].astype(F32)


def branch_kernel(pair_hbm, carried_ref, w_ref, out_hbm, q_ref, local_ref, normed_ref, out_ref, in_sem, sem):
    rows = out_ref.shape[0]
    in_copies = slab_copies(
        (pair_hbm.at[pl.ds(0, rows)], pair_hbm.at[pl.ds(rows, rows)]), (q_ref, local_ref), in_sem
    )
    for slab in in_copies:
        for copy in slab:
            copy.start()
    for h in range(HEADS):
        if h % SLAB == 0:
            for copy in in_copies[h // SLAB]:
                copy.wait()
        mixed = local_ref[:, head(h)].astype(F32) + jnp.dot(
            q_ref[:, head(h)], carried_ref[head(h), :], preferred_element_type=F32
        )
        scale = lax.rsqrt(jnp.mean(mixed * mixed, axis=1, keepdims=True) + EPSILON)
        normed_ref[:, head(h)] = (mixed * scale).astype(BF16)
    middle = (rows // 2 + 15) // 16 * 16
    copies = []
    for n, (low, high) in enumerate(((0, middle), (middle, rows))):
        part = pl.ds(low, high - low)
        out_ref[part, :] = jnp.dot(
            normed_ref[part, :], w_ref[...], preferred_element_type=F32
        ).astype(BF16)
        copies.append(pltpu.make_async_copy(out_ref.at[part], out_hbm.at[part], sem.at[n]))
        copies[n].start()
    for copy in copies:
        copy.wait()


def handed_on(array):
    size = lax.axis_size("segment")
    return lax.ppermute(array, "segment", [((i - 1) % size, i) for i in range(size)])


def shards(queries, key_rows, value_rows, out_weight):
    q, k, v, w = queries[0], key_rows[0], value_rows[0], out_weight[0]
    rows, width = q.shape
    blocks = lax.axis_size("seq")
    near = [[g * GROUP + m for m in range(GROUP)] for g in range(blocks // GROUP)]
    piece = (HEADS * HEAD_DIM // GROUP, HEAD_DIM)
    block = pltpu.VMEM((rows, width), BF16)
    sems = lambda n: pltpu.SemaphoreType.DMA((HEADS // SLAB, n))

    states = call(
        states_kernel, jax.ShapeDtypeStruct((HEADS * HEAD_DIM, HEAD_DIM), BF16), (k, v), [ANY] * 2,
        2 * rows * width * HEAD_DIM, 2 * rows * width * 2, limit=60 << 20, scratch=[block, block, sems(2)],
    )
    states_next = handed_on(states)
    pair = call(
        local_kernel, jax.ShapeDtypeStruct((2 * rows, width), BF16), (q, k, v, states), [ANY] * 4,
        4 * rows * rows * width, 5 * rows * width * 2, limit=60 << 20, scratch=[block, block, sems(3)],
    )
    states_next, w, pair = lax.optimization_barrier((states_next, w, pair))
    w_next, pair_next = handed_on(w), handed_on(pair)
    slices = lax.all_to_all(states_next.reshape(GROUP, *piece), "seq", 0, 0, axis_index_groups=near)
    total = call(
        total_kernel, jax.ShapeDtypeStruct(piece, F32), (slices,), [VMEM], 1 << 17, 1 << 19, limit=4 << 20,
    )
    groups = blocks // GROUP
    order = sorted(range(1, groups), key=lambda d: min(d, groups - d))
    totals = [
        lax.ppermute(total, "seq", [(i, i + d * GROUP) for i in range(blocks - d * GROUP)])
        for d in order
    ]
    prefixes = call(
        prefix_kernel, jax.ShapeDtypeStruct((GROUP, *piece), BF16), (slices, *totals),
        [VMEM] * (1 + len(totals)), 1 << 18, 1 << 20, limit=4 << 20,
    )
    carried = lax.all_to_all(prefixes, "seq", 0, 0, axis_index_groups=near).reshape(-1, HEAD_DIM)
    branch = call(
        branch_kernel, jax.ShapeDtypeStruct((rows, width), BF16), (pair_next, carried, w_next), [ANY, VMEM, VMEM],
        2 * rows * width * (width + HEAD_DIM), 6 << 20, out_specs=ANY, limit=16 << 20,
        scratch=[block, block, block, block, sems(2), pltpu.SemaphoreType.DMA((2,))],
    )
    return branch[None]


def solution(mesh):
    return jax.shard_map(
        shards,
        mesh=mesh,
        in_specs=(
            P("segment", "seq", None),
            P("segment", "seq", None),
            P("segment", "seq", None),
            P("segment", None, None),
        ),
        out_specs=P("segment", "seq", None),
        check_vma=False,
    )
```
